256 devices in a mesh: blk: 32 (over z, y), aux: 8 (over x, core).
Axes of the slice: x: 4, y: 4, z: 8, core: 2. Of those that a mesh axis runs over, the one named last changes fastest.
Arguments:
- pair_cols: int32 [32, 16], P('blk'), may hold values from 0 to 31, as said below
- pair_count: int32 [32], P('blk'), may hold values from 1 to 16, as said below
- integrals: bfloat16 [512, 32, 128, 128], P('blk', 'aux'), may hold values from -1 to 1
- coeffs: bfloat16 [4096, 512], P('blk'), may hold values from -8 to 8
Outputs:
- exchange: float32 [4096, 4096], P('blk', 'aux')
The draws below stay inside these ranges and needn't reach their ends.
Inputs may be any that keep to these rules, and one draw needn't show every extreme that they name: `pair_cols`: entry s of row M is M for s = 0; within a row all entries are distinct blocks. `pair_count`: some row block lists all 16 slots.
All inputs are finite; a program needn't handle non-finite values.
Results may differ from the reference program's by a relative error of at most 0.00072.
Values may be sent and summed in bfloat16 or wider, within the bound.
No kernel may reach another device: no remote copies, remote signals or barrier semaphores. Data moves between devices by JAX's collectives and lax.ppermute only.
A program may use at most 64 MiB of HBM per device.

```python
import math
import jax
import jax.numpy as jnp
from jax import lax

BLOCK = 128
NOCC = 512
AUX = 32
NBF = 4096
SLOTS = 16
N_BLK = 32


def draw_pair_cols(key, part):
    key = jax.random.fold_in(key, 11)
    row_keys = jax.random.split(key, N_BLK)

    def one_row(row_key, owner):
        shuffled = jax.random.permutation(row_key, N_BLK - 1).astype(jnp.int32)
        others = (owner + 1 + shuffled) % N_BLK
        return jnp.concatenate([jnp.reshape(owner, (1,)), others[:SLOTS - 1]]).astype(jnp.int32)
    return jax.vmap(one_row)(row_keys, jnp.arange(N_BLK, dtype=jnp.int32))


def draw_pair_count(key, part):
    key = jax.random.fold_in(key, 12)
    first_key, second_key = jax.random.split(key)
    counts = jax.random.randint(first_key, (N_BLK,), 1, SLOTS // 2 + 1).astype(jnp.int32)
    busiest = jax.random.randint(second_key, (), 0, N_BLK).astype(jnp.int32)
    filled = jnp.full((N_BLK,), SLOTS, jnp.int32)
    return jnp.where(jnp.arange(N_BLK, dtype=jnp.int32) == busiest, filled, counts)


def normal_part(key, shape, limit):
    return jnp.clip(jax.random.normal(key, shape, jnp.float32), -limit, limit)


def draw_integrals(key, part):
    key = jax.random.fold_in(key, 13)
    own_key, single_key, common_key = jax.random.split(key, 3)
    scale = 1.0 / math.sqrt(4.0 * BLOCK)
    own = normal_part(own_key, (N_BLK * SLOTS, AUX, BLOCK, BLOCK), 4.0)
    single = normal_part(single_key, (AUX, BLOCK, BLOCK), 4.0)
    common = normal_part(common_key, (AUX, 1, BLOCK), 4.0)
    shared = 0.8 * (single + 0.6 * common)
    return jnp.clip(scale * (own + shared[None]), -1.0, 1.0).astype(jnp.bfloat16)


def draw_coeffs(key, part):
    key = jax.random.fold_in(key, 14)
    own_key, common_key, sign_key, size_key = jax.random.split(key, 4)
    signs = (2 * jax.random.randint(sign_key, (N_BLK, 1, 1), 0, 2) - 1).astype(jnp.float32)
    factors = signs * jax.random.uniform(size_key, (N_BLK, 1, 1), jnp.float32, 0.6, 1.4)
    own = normal_part(own_key, (N_BLK, BLOCK, NOCC), 4.0)
    common = normal_part(common_key, (1, BLOCK, NOCC), 4.0)
    return jnp.clip(own + factors * common, -8.0, 8.0).reshape(N_BLK * BLOCK, NOCC).astype(jnp.bfloat16)


def setup_inputs(seed: int = 0) -> dict:
    keys = jax.random.split(jax.random.key(seed), 5)
    return {
        "pair_cols": draw_pair_cols(jax.random.fold_in(keys[4], 71), 0),
        "pair_count": draw_pair_count(jax.random.fold_in(keys[4], 71), 0),
        "integrals": draw_integrals(jax.random.fold_in(keys[4], 71), 0),
        "coeffs": draw_coeffs(jax.random.fold_in(keys[4], 71), 0),
    }


def reference(pair_cols, pair_count, integrals, coeffs):
    coeff_blocks = coeffs.reshape(N_BLK, BLOCK, NOCC)
    tiled = integrals.reshape(N_BLK, SLOTS, AUX, BLOCK, BLOCK)

    def block_halfway(operands):
        block_tiles, columns, counted = operands
        coeff_rows = jnp.take(coeff_blocks, columns.astype(jnp.int32), axis=0)
        live_slots = (jnp.arange(SLOTS, dtype=jnp.int32) < counted).astype(jnp.float32)
        summed = jnp.einsum('s,spml,sli->pmi', live_slots, block_tiles.astype(jnp.float32), coeff_rows.astype(jnp.float32))
        return summed.astype(jnp.bfloat16)
    halfway = lax.map(block_halfway, (tiled, pair_cols, pair_count))
    flat = halfway.transpose(0, 2, 1, 3).reshape(NBF, AUX * NOCC)
    scale = 1.0 / math.sqrt(AUX * NOCC)
    return jnp.dot(flat, flat.T, preferred_element_type=jnp.float32) * scale
```

```python
import math

import jax
import jax.numpy as jnp
from jax import lax
from jax.experimental import pallas as pl
from jax.experimental.pallas import tpu as pltpu
from jax.sharding import Mesh, PartitionSpec as P

NZ, NY, NX, NC = 8, 4, 4, 2
SLOTS, BLOCK, NOCC, AUX_HERE = 16, 128, 512, 4
HALF_L = BLOCK // NC
SLICE = NOCC // NX
LIMIT = 40 * 1024 * 1024

VMEM = pl.BlockSpec(memory_space=pltpu.VMEM)
SMEM = pl.BlockSpec(memory_space=pltpu.SMEM)


def shift(x, axis, size, step):
    return lax.ppermute(x, axis, [(i, (i + step) % size) for i in range(size)])


def pick_kernel(cols, count, gathered, out):
    counted = count[0]
    for s in range(SLOTS):
        rows = gathered[cols[0, s]]
        out[s] = jnp.where(s < counted, rows, jnp.zeros_like(rows))


def pick(cols, count, gathered):
    return pl.pallas_call(
        pick_kernel,
        out_shape=jax.ShapeDtypeStruct((SLOTS, HALF_L, SLICE), jnp.bfloat16),
        in_specs=[SMEM, SMEM, VMEM],
        out_specs=VMEM,
        compiler_params=pltpu.CompilerParams(vmem_limit_bytes=LIMIT),
    )(cols, count, gathered)


def half_kernel(core, integrals, *refs):
    mine, other, out = refs[:NX], refs[NX:2 * NX], refs[2 * NX]
    first = core[0] == 0
    left = jnp.concatenate(
        [integrals[s].reshape(AUX_HERE * BLOCK, BLOCK) for s in range(SLOTS)], axis=1
    )
    for h in range(2):
        parts = []
        for d in (2 * h, 2 * h + 1):
            a, b = mine[d][...], other[d][...]
            top, low = jnp.where(first, a, b), jnp.where(first, b, a)
            parts.append(jnp.concatenate([top, low], axis=1).reshape(SLOTS * BLOCK, SLICE))
        right = jnp.concatenate(parts, axis=1)
        done = jnp.dot(left, right, preferred_element_type=jnp.float32).astype(jnp.bfloat16)
        for p in range(AUX_HERE):
            out[h, :, p * 2 * SLICE:(p + 1) * 2 * SLICE] = done[p * BLOCK:(p + 1) * BLOCK]


def half_transform(core, integrals, mine, other):
    return pl.pallas_call(
        half_kernel,
        out_shape=jax.ShapeDtypeStruct((2, BLOCK, AUX_HERE * 2 * SLICE), jnp.bfloat16),
        in_specs=[SMEM] + [VMEM] * (1 + 2 * NX),
        out_specs=VMEM,
        compiler_params=pltpu.CompilerParams(vmem_limit_bytes=LIMIT),
    )(core, integrals, *mine, *other)


def tile_kernel(place, *refs):
    out = refs[-1]
    g0, gm, gp, g2a, g2b = refs[:5]
    v = refs[5:-1]
    z, y, core = place[0], place[1], place[2]
    rows = [
        jnp.concatenate([g0[0], gm[0], gp[0], g2a[...]], axis=0),
        jnp.concatenate([g0[1], gm[1], gp[1], g2b[...]], axis=0),
    ]
    row_at = [y, lax.rem(y + 3, NY), lax.rem(y + 1, NY), lax.rem(y + 2, NY)]
    pairs = [
        ((v[1], v[2]), (-1, 1)),
        ((v[3], v[4]), (-2, 2)),
        ((v[5], v[6]), (-3, 3)),
        ((v[0], None), (0, 4)),
    ]
    dims = (((1,), (1,)), ((), ()))
    for (a, b), offsets in pairs:
        total = None
        for h in range(2):
            second = b[h] if b is not None else v[7 + h][...]
            columns = jnp.concatenate([a[h], second], axis=0)
            term = lax.dot_general(rows[h], columns, dims, preferred_element_type=jnp.float32)
            total = term if total is None else total + term
        for n, offset in enumerate(offsets):
            at = lax.rem(z + offset + NZ, NZ)
            x_at, side = lax.div(at, NC), lax.rem(lax.rem(at, NC) + core, NC)
            for r in range(NY):
                out[side, row_at[r] * NX + x_at] = total[
                    r * BLOCK:(r + 1) * BLOCK, n * BLOCK:(n + 1) * BLOCK
                ]


def tile_product(place, rows, columns):
    return pl.pallas_call(
        tile_kernel,
        out_shape=jax.ShapeDtypeStruct((NC, NY * NX, BLOCK, BLOCK), jnp.float32),
        in_specs=[SMEM] + [VMEM] * (len(rows) + len(columns)),
        out_specs=VMEM,
        compiler_params=pltpu.CompilerParams(vmem_limit_bytes=LIMIT),
    )(place, *rows, *columns)


def finish_kernel(scale, parts, out):
    for yy in range(NY):
        total = parts[yy * NX]
        for xx in range(1, NX):
            total = total + parts[yy * NX + xx]
        out[:, yy * BLOCK:(yy + 1) * BLOCK] = total * scale


def finish(parts, scale):
    def body(parts_ref, out):
        finish_kernel(scale, parts_ref, out)

    return pl.pallas_call(
        body,
        out_shape=jax.ShapeDtypeStruct((BLOCK, NY * BLOCK), jnp.float32),
        in_specs=[VMEM],
        out_specs=VMEM,
        compiler_params=pltpu.CompilerParams(vmem_limit_bytes=LIMIT),
    )(parts)


def shards(pair_cols, pair_count, integrals, coeffs):
    z, y = lax.axis_index("z"), lax.axis_index("y")
    x, core = lax.axis_index("x"), lax.axis_index("core")

    piece = lax.dynamic_slice(coeffs, (core * HALF_L, x * SLICE), (HALF_L, SLICE))
    gathered = lax.all_to_all(
        jnp.broadcast_to(piece[None], (NZ * NY, HALF_L, SLICE)), ("z", "y"), 0, 0, tiled=True
    )
    picked = pick(pair_cols, pair_count, gathered)
    mine = [picked] + [shift(picked, "x", NX, d) for d in (1, 3, 2)]
    other = [shift(m, "core", NC, 1) for m in mine]
    halfway = half_transform(core[None], integrals, mine, other)

    y_up, y_down = shift(halfway, "y", NY, 1), shift(halfway, "y", NY, -1)
    y_far = [shift(y_up[0], "y", NY, 1), shift(y_down[1], "y", NY, -1)]
    rows = [halfway, y_up, y_down] + y_far
    columns = [halfway]
    up = down = halfway
    for _ in range(3):
        up, down = shift(up, "z", NZ, 1), shift(down, "z", NZ, -1)
        columns += [up, down]
    columns += [shift(up[0], "z", NZ, 1), shift(down[1], "z", NZ, -1)]
    place = jnp.stack([z, y, core]).astype(jnp.int32)
    tile = tile_product(place, rows, columns)

    both = tile[0] + shift(tile[1], "core", NC, 1)
    parts = lax.all_to_all(both, ("y", "x"), 0, 0, tiled=True)
    scale = 1.0 / math.sqrt(AUX_HERE * NX * NC * NOCC)
    return finish(parts, scale)


def solution(mesh):
    grid = Mesh(mesh.devices.reshape(NZ, NY, NX, NC), ("z", "y", "x", "core"))
    blk, aux = ("z", "y"), ("x", "core")
    placed = (P(blk, None), P(blk), P(blk, aux, None, None), P(blk, None))
    return jax.shard_map(
        shards, mesh=grid, in_specs=placed, out_specs=P(blk, aux), check_vma=False
    )
```

```python
import functools
import math

import jax
import jax.numpy as jnp
from jax import lax
from jax.experimental import pallas as pl
from jax.experimental.pallas import tpu as pltpu
from jax.sharding import Mesh, PartitionSpec as P

NZ, NY, NX, NC = 8, 4, 4, 2
SLOTS, BLOCK, NOCC, AUX_HERE = 16, 128, 512, 4
HALF_L = BLOCK // NC
SLICE = NOCC // NX
CHUNK = AUX_HERE * SLICE
ROWS = AUX_HERE * BLOCK
LIMIT = 24 * 1024 * 1024
VMEM = pl.BlockSpec(memory_space=pltpu.VMEM)
SMEM = pl.BlockSpec(memory_space=pltpu.SMEM)


def call(body, out_shape, scalars, arrays, flops=None, aliases=None):
    return pl.pallas_call(
        body,
        out_shape=out_shape,
        in_specs=[SMEM] * len(scalars) + [VMEM] * len(arrays),
        out_specs=jax.tree.map(lambda _: VMEM, out_shape),
        cost_estimate=flops and pl.CostEstimate(flops=flops, bytes_accessed=12000000, transcendentals=0),
        input_output_aliases=aliases or {},
        compiler_params=pltpu.CompilerParams(vmem_limit_bytes=LIMIT),
    )(*scalars, *arrays)


def bf16(*shape):
    return jax.ShapeDtypeStruct(shape, jnp.bfloat16)


def shift(x, axis, size, step):
    return lax.ppermute(x, axis, [(i, (i + step) % size) for i in range(size)])


def mirrored(x, axis, size, step):
    pairs = []
    for i in range(size):
        pairs.append((i * NC, (i + step) % size * NC))
        pairs.append((i * NC + 1, (i - step) % size * NC + 1))
    return lax.ppermute(x, (axis, "core"), pairs)


def swap_cores(x):
    return shift(x, "core", NC, 1)


def pick_kernel(info, *refs):
    gathered, out = refs[:NY], refs[NY]
    counted, y = info[SLOTS], info[SLOTS + 1]
    for s in range(SLOTS):
        column = info[s]
        z_at, y_at = lax.div(column, NY), lax.rem(column, NY)
        from_y = lax.rem(y - y_at + NY, NY)
        rows = gathered[0][z_at]
        for d in range(1, NY):
            rows = jnp.where(from_y == d, gathered[d][z_at], rows)
        out[s] = jnp.where(s < counted, rows, jnp.zeros_like(rows))


def load_kernel(source, out, done):
    copy = pltpu.make_async_copy(source, out, done)
    copy.start()
    copy.wait()


def load(source):
    return pl.pallas_call(
        load_kernel,
        out_shape=jax.ShapeDtypeStruct(source.shape, source.dtype),
        in_specs=[pl.BlockSpec(memory_space=pl.ANY)],
        out_specs=VMEM,
        scratch_shapes=[pltpu.SemaphoreType.DMA],
        compiler_params=pltpu.CompilerParams(vmem_limit_bytes=LIMIT),
    )(source)


def half(core, integrals, mine, other):
    first = core[0] == 0
    left = jnp.concatenate(
        [integrals[s].reshape(ROWS, BLOCK) for s in range(SLOTS)], axis=1
    )
    parts = []
    for m, o in zip(mine, other):
        a, b = m[...], o[...]
        top, low = jnp.where(first, a, b), jnp.where(first, b, a)
        parts.append(jnp.concatenate([top, low], axis=1).reshape(SLOTS * BLOCK, SLICE))
    right = parts[0] if len(parts) == 1 else jnp.concatenate(parts, axis=1)
    return jnp.dot(left, right, preferred_element_type=jnp.float32).astype(jnp.bfloat16)


def half_kernel(core, integrals, *refs):
    out = refs[-1]
    done = half(core, integrals, refs[:NX], refs[NX:2 * NX])
    for p in range(AUX_HERE):
        at = slice(p % 2 * NOCC, (p % 2 + 1) * NOCC)
        out[p // 2, :, at] = done[p * BLOCK:(p + 1) * BLOCK]


def place_of(place, offset):
    z, core = place[0], place[2]
    at = lax.rem(z + offset + NZ, NZ)
    return lax.div(at, NC), lax.rem(lax.rem(at, NC) + core, NC)


def times(rows, columns):
    return lax.dot_general(
        rows, columns, (((1,), (1,)), ((), ())), preferred_element_type=jnp.float32
    )


def row_places(place):
    y, sign = place[1], 1 - 2 * place[2]
    return [y] + [lax.rem(y + d * sign + NY, NY) for d in (-1, 1, 2)]


def put(place, out, total, offsets):
    row_at = row_places(place)
    for n, offset in enumerate(offsets):
        x_at, side = place_of(place, offset)
        for r in range(NY):
            at = row_at[r] * NX + x_at
            out[side, at] = total[r * BLOCK:(r + 1) * BLOCK, n * BLOCK:(n + 1) * BLOCK]


def product(grows, blocks):
    total = None
    for h in range(2):
        rows = jnp.concatenate([g[h] for g in grows], axis=0)
        columns = [block[h][0] for block in blocks]
        columns = columns[0] if len(columns) == 1 else jnp.concatenate(columns, axis=0)
        term = times(rows, columns)
        total = term if total is None else total + term
    return total


def first_kernel(place, *refs):
    grows, out = refs[:4], refs[4]
    own = grows[0]
    put(place, out, product(grows, [(own.at[pl.ds(0, 1)], own.at[pl.ds(1, 1)])]), (0,))


def pair_kernel(k, place, *refs):
    grows, columns, out = refs[:4], refs[4:8], refs[9]
    put(place, out, product(grows, [columns[0:2], columns[2:4]]), (-k, k))


def last_kernel(place, *refs):
    grows, columns, out = refs[:4], refs[4:8], refs[9]
    total = None
    for h in range(2):
        rows = jnp.concatenate([g[h] for g in grows], axis=0)
        block = jnp.concatenate([columns[2 * h][0], columns[2 * h + 1][0]], axis=0)
        term = times(rows, block)
        total = term if total is None else total + term
    put(place, out, total, (4,))


def finish_kernel(parts, out):
    scale = 1.0 / math.sqrt(AUX_HERE * NX * NC * NOCC)
    for yy in range(NY):
        total = parts[yy * NX]
        for xx in range(1, NX):
            total = total + parts[yy * NX + xx]
        out[:, yy * BLOCK:(yy + 1) * BLOCK] = total * scale


def shards(pair_cols, pair_count, integrals, coeffs):
    z, y = lax.axis_index("z"), lax.axis_index("y")
    x, core = lax.axis_index("x"), lax.axis_index("core")
    core_at = core[None].astype(jnp.int32)
    place = jnp.stack([z, y, core]).astype(jnp.int32)

    info = jnp.concatenate([pair_cols[0], pair_count, y[None].astype(jnp.int32)])
    loaded = load(integrals)

    piece = lax.dynamic_slice(coeffs, (core * HALF_L, x * SLICE), (HALF_L, SLICE))
    along_z = lax.all_to_all(
        jnp.broadcast_to(piece[None], (NZ, HALF_L, SLICE)), "z", 0, 0, tiled=True
    )
    along_z, loaded, info = lax.optimization_barrier((along_z, loaded, info))
    gathered = [along_z] + [shift(along_z, "y", NY, d) for d in (1, 2, 3)]
    picked = call(
        pick_kernel, bf16(SLOTS, HALF_L, SLICE),
        [info], gathered,
    )
    slices = [picked] + [shift(picked, "x", NX, d) for d in (1, 3, 2)]
    halfway = call(
        half_kernel, bf16(2, BLOCK, 2 * CHUNK), [core_at], [loaded] + slices + [swap_cores(m) for m in slices]
    )
    halves = [lax.slice_in_dim(halfway, h, h + 1, axis=0) for h in range(2)]
    ups, downs = list(halves), list(halves)
    y_a, y_b = mirrored(halfway, "y", NY, 1), mirrored(halfway, "y", NY, -1)
    y_far = mirrored(y_a, "y", NY, 1)
    columns = []
    for step in range(3):
        for h in range(2):
            up, down = shift(ups[h], "z", NZ, 1), shift(downs[h], "z", NZ, -1)
            if h == 1 and step == 1:
                up, down, y_a, y_b = lax.optimization_barrier((up, down, y_a, y_b))
            ups[h], downs[h] = up, down
        columns.append([(ups[0], ups[1]), (downs[0], downs[1])])
    last = []
    for h in range(2):
        low = shift(ups[h][:, :BLOCK // 2], "z", NZ, 1)
        high = shift(downs[h][:, BLOCK // 2:], "z", NZ, -1)
        last.append((low, high))
    rows = [halfway, y_a, y_b, y_far]

    tiles = jax.ShapeDtypeStruct((NC, NY * NX, BLOCK, BLOCK), jnp.float32)
    tile = call(first_kernel, tiles, [place], rows, flops=270000000)
    for k in range(3):
        blocks = [half for pair in columns[k] for half in pair]
        tile = call(
            functools.partial(pair_kernel, k + 1), tiles, [place], rows + blocks + [tile],
            flops=540000000, aliases={9: 0},
        )
    blocks = [half for pair in last for half in pair]
    tile = call(last_kernel, tiles, [place], rows + blocks + [tile], aliases={9: 0})

    both = tile[0] + swap_cores(tile[1])
    parts = lax.all_to_all(both, ("y", "x"), 0, 0, tiled=True)
    return call(
        finish_kernel, jax.ShapeDtypeStruct((BLOCK, NY * BLOCK), jnp.float32), [], [parts]
    )


def solution(mesh):
    grid = Mesh(mesh.devices.reshape(NZ, NY, NX, NC), ("z", "y", "x", "core"))
    blk, aux = ("z", "y"), ("x", "core")
    placed = (P(blk, None), P(blk), P(blk, aux, None, None), P(blk, None))
    return jax.shard_map(
        shards, mesh=grid, in_specs=placed, out_specs=P(blk, aux), check_vma=False
    )
```

```python
import functools
import math

import jax
import jax.numpy as jnp
from jax import lax
from jax.experimental import pallas as pl
from jax.experimental.pallas import tpu as pltpu
from jax.sharding import Mesh, PartitionSpec as P

NZ, NY, NX, NC = 8, 4, 4, 2
SLOTS, BLOCK, NOCC, AUX_HERE = 16, 128, 512, 4
HALF_L = BLOCK // NC
SLICE = NOCC // NX
CHUNK = AUX_HERE * SLICE
ROWS = AUX_HERE * BLOCK
STEPS, PAD = 32000.0, 16
LIMIT = 24 * 1024 * 1024
VMEM = pl.BlockSpec(memory_space=pltpu.VMEM)
SMEM = pl.BlockSpec(memory_space=pltpu.SMEM)


def call(body, out_shape, scalars, arrays, flops=None, aliases=None):
    return pl.pallas_call(
        body,
        out_shape=out_shape,
        in_specs=[SMEM] * len(scalars) + [VMEM] * len(arrays),
        out_specs=jax.tree.map(lambda _: VMEM, out_shape),
        cost_estimate=flops and pl.CostEstimate(flops=flops, bytes_accessed=12000000, transcendentals=0),
        input_output_aliases=aliases or {},
        compiler_params=pltpu.CompilerParams(vmem_limit_bytes=LIMIT),
    )(*scalars, *arrays)


def bf16(*shape):
    return jax.ShapeDtypeStruct(shape, jnp.bfloat16)


def shift(x, axis, size, step):
    return lax.ppermute(x, axis, [(i, (i + step) % size) for i in range(size)])


def mirrored(x, axis, size, step):
    pairs = []
    for i in range(size):
        pairs.append((i * NC, (i + step) % size * NC))
        pairs.append((i * NC + 1, (i - step) % size * NC + 1))
    return lax.ppermute(x, (axis, "core"), pairs)


def swap_cores(x):
    return shift(x, "core", NC, 1)


def pick_kernel(info, *refs):
    gathered, out = refs[:NY], refs[NY]
    counted, y = info[SLOTS], info[SLOTS + 1]
    for s in range(SLOTS):
        column = info[s]
        z_at, y_at = lax.div(column, NY), lax.rem(column, NY)
        from_y = lax.rem(y - y_at + NY, NY)
        rows = gathered[0][z_at]
        for d in range(1, NY):
            rows = jnp.where(from_y == d, gathered[d][z_at], rows)
        out[s] = jnp.where(s < counted, rows, jnp.zeros_like(rows))


def load_kernel(source, out, done):
    copy = pltpu.make_async_copy(source, out, done)
    copy.start()
    copy.wait()


def load(source):
    return pl.pallas_call(
        load_kernel,
        out_shape=jax.ShapeDtypeStruct(source.shape, source.dtype),
        in_specs=[pl.BlockSpec(memory_space=pl.ANY)],
        out_specs=VMEM,
        scratch_shapes=[pltpu.SemaphoreType.DMA],
        compiler_params=pltpu.CompilerParams(vmem_limit_bytes=LIMIT),
    )(source)


def half(core, integrals, mine, other):
    first = core[0] == 0
    left = jnp.concatenate(
        [integrals[s].reshape(ROWS, BLOCK) for s in range(SLOTS)], axis=1
    )
    parts = []
    for m, o in zip(mine, other):
        a, b = m[...], o[...]
        top, low = jnp.where(first, a, b), jnp.where(first, b, a)
        parts.append(jnp.concatenate([top, low], axis=1).reshape(SLOTS * BLOCK, SLICE))
    right = parts[0] if len(parts) == 1 else jnp.concatenate(parts, axis=1)
    return jnp.dot(left, right, preferred_element_type=jnp.float32).astype(jnp.bfloat16)


def half_kernel(core, integrals, *refs):
    out = refs[-1]
    done = half(core, integrals, refs[:NX], refs[NX:2 * NX])
    for p in range(AUX_HERE):
        at = slice(p % 2 * NOCC, (p % 2 + 1) * NOCC)
        out[p // 2, :, at] = done[p * BLOCK:(p + 1) * BLOCK]


def place_of(place, offset):
    z, core = place[0], place[2]
    at = lax.rem(z + offset + NZ, NZ)
    return lax.div(at, NC), lax.rem(lax.rem(at, NC) + core, NC)


def times(rows, columns):
    return lax.dot_general(
        rows, columns, (((1,), (1,)), ((), ())), preferred_element_type=jnp.float32
    )


def row_places(place):
    y, sign = place[1], 1 - 2 * place[2]
    return [y] + [lax.rem(y + d * sign + NY, NY) for d in (-1, 1, 2)]


def put(place, out, total, offsets):
    row_at = row_places(place)
    for n, offset in enumerate(offsets):
        x_at, side = place_of(place, offset)
        for r in range(NY):
            at = row_at[r] * NX + x_at
            out[side, at] = total[r * BLOCK:(r + 1) * BLOCK, n * BLOCK:(n + 1) * BLOCK]


def product(grows, blocks):
    total = None
    for h in range(2):
        rows = jnp.concatenate([g[h] for g in grows], axis=0)
        columns = [block[h][0] for block in blocks]
        columns = columns[0] if len(columns) == 1 else jnp.concatenate(columns, axis=0)
        term = times(rows, columns)
        total = term if total is None else total + term
    return total


def first_kernel(place, *refs):
    grows, out = refs[:4], refs[4]
    own = grows[0]
    put(place, out, product(grows, [(own.at[pl.ds(0, 1)], own.at[pl.ds(1, 1)])]), (0,))


def early_kernel(place, *refs):
    grows, columns, out = refs[:4], refs[4:12], refs[13]
    blocks = [columns[2 * n:2 * n + 2] for n in range(4)]
    put(place, out, product(grows, blocks), (-1, 1, -2, 2))


def late_kernel(place, *refs):
    grows, columns, out = refs[:4], refs[4:12], refs[13]
    put(place, out, product(grows, [columns[0:2], columns[2:4]]), (-3, 3))
    total = None
    for h in range(2):
        rows = jnp.concatenate([g[h] for g in grows], axis=0)
        block = jnp.concatenate([columns[4 + 2 * h][0], columns[5 + 2 * h][0]], axis=0)
        term = times(rows, block)
        total = term if total is None else total + term
    put(place, out, total, (4,))


def encode_kernel(kept, got, out):
    for n in range(NY * NX):
        total = kept[0, n] + got[n]
        top = jnp.maximum(jnp.max(jnp.abs(total), axis=0, keepdims=True), 2.0 ** -120)
        power = jnp.ceil(jnp.log2(top))
        scaled = jnp.floor(total * jnp.exp2(-power) * STEPS + 0.5)
        out[n, :BLOCK] = scaled.astype(jnp.int32).astype(jnp.int16)
        power = jnp.broadcast_to(power, (PAD, BLOCK))
        out[n, BLOCK:] = power.astype(jnp.int32).astype(jnp.int16)


def finish_kernel(parts, out):
    scale = 1.0 / math.sqrt(AUX_HERE * NX * NC * NOCC) / STEPS
    for yy in range(NY):
        total = None
        for xx in range(NX):
            part = parts.at[yy * NX + xx]
            power = part[BLOCK:].astype(jnp.int32).astype(jnp.float32)[:1]
            term = part[:BLOCK].astype(jnp.int32).astype(jnp.float32) * (jnp.exp2(power) * scale)
            total = term if total is None else total + term
        out[:, yy * BLOCK:(yy + 1) * BLOCK] = total


def shards(pair_cols, pair_count, integrals, coeffs):
    z, y = lax.axis_index("z"), lax.axis_index("y")
    x, core = lax.axis_index("x"), lax.axis_index("core")
    core_at = core[None].astype(jnp.int32)
    place = jnp.stack([z, y, core]).astype(jnp.int32)

    info = jnp.concatenate([pair_cols[0], pair_count, y[None].astype(jnp.int32)])
    loaded = load(integrals)

    piece = lax.dynamic_slice(coeffs, (core * HALF_L, x * SLICE), (HALF_L, SLICE))
    along_z = lax.all_to_all(
        jnp.broadcast_to(piece[None], (NZ, HALF_L, SLICE)), "z", 0, 0, tiled=True
    )
    along_z, loaded, info = lax.optimization_barrier((along_z, loaded, info))
    gathered = [along_z] + [shift(along_z, "y", NY, d) for d in (1, 2, 3)]
    picked = call(
        pick_kernel, bf16(SLOTS, HALF_L, SLICE),
        [info], gathered,
    )
    slices = [picked] + [shift(picked, "x", NX, d) for d in (1, 3, 2)]
    halfway = call(
        half_kernel, bf16(2, BLOCK, 2 * CHUNK), [core_at], [loaded] + slices + [swap_cores(m) for m in slices]
    )
    halves = [lax.slice_in_dim(halfway, h, h + 1, axis=0) for h in range(2)]
    ups, downs = list(halves), list(halves)
    y_a, y_b = mirrored(halfway, "y", NY, 1), mirrored(halfway, "y", NY, -1)
    y_far = mirrored(y_a, "y", NY, 1)
    columns = []
    for step in range(3):
        for h in range(2):
            up, down = shift(ups[h], "z", NZ, 1), shift(downs[h], "z", NZ, -1)
            if h == 1 and step == 1:
                up, down, y_a, y_b = lax.optimization_barrier((up, down, y_a, y_b))
            ups[h], downs[h] = up, down
        columns.append([(ups[0], ups[1]), (downs[0], downs[1])])
    last = []
    for h in range(2):
        low = shift(ups[h][:, :BLOCK // 2], "z", NZ, 1)
        high = shift(downs[h][:, BLOCK // 2:], "z", NZ, -1)
        last.append((low, high))
    rows = [halfway, y_a, y_b, y_far]

    tiles = jax.ShapeDtypeStruct((NC, NY * NX, BLOCK, BLOCK), jnp.float32)
    def blocks(pairs):
        return [half for pair in pairs for half in pair]

    tile = call(first_kernel, tiles, [place], rows, flops=270000000)
    tile = call(
        early_kernel, tiles, [place], rows + blocks(columns[0] + columns[1]) + [tile],
        flops=1080000000, aliases={13: 0},
    )
    tile = call(late_kernel, tiles, [place], rows + blocks(columns[2] + last) + [tile], aliases={13: 0})

    coded = call(
        encode_kernel, jax.ShapeDtypeStruct((NY * NX, BLOCK + PAD, BLOCK), jnp.int16), [],
        [tile, swap_cores(tile[1])],
    )
    parts = lax.all_to_all(coded, ("y", "x"), 0, 0, tiled=True)
    return call(
        finish_kernel, jax.ShapeDtypeStruct((BLOCK, NY * BLOCK), jnp.float32), [], [parts]
    )


def solution(mesh):
    grid = Mesh(mesh.devices.reshape(NZ, NY, NX, NC), ("z", "y", "x", "core"))
    blk, aux = ("z", "y"), ("x", "core")
    placed = (P(blk, None), P(blk), P(blk, aux, None, None), P(blk, None))
    return jax.shard_map(
        shards, mesh=grid, in_specs=placed, out_specs=P(blk, aux), check_vma=False
    )
```

```python
import functools
import math

import jax
import jax.numpy as jnp
from jax import lax
from jax.experimental import pallas as pl
from jax.experimental.pallas import tpu as pltpu
from jax.sharding import Mesh, PartitionSpec as P

NZ, NY, NX, NC = 8, 4, 4, 2
SLOTS, BLOCK, NOCC, AUX_HERE = 16, 128, 512, 4
HALF_L = BLOCK // NC
SLICE = NOCC // NX
CHUNK = AUX_HERE * SLICE
ROWS = AUX_HERE * BLOCK
STEPS, PAD = 32000.0, 16
LIMIT = 24 * 1024 * 1024
VMEM = pl.BlockSpec(memory_space=pltpu.VMEM)
SMEM = pl.BlockSpec(memory_space=pltpu.SMEM)


def call(body, out_shape, scalars, arrays, flops=None, aliases=None):
    return pl.pallas_call(
        body,
        out_shape=out_shape,
        in_specs=[SMEM] * len(scalars) + [VMEM] * len(arrays),
        out_specs=jax.tree.map(lambda _: VMEM, out_shape),
        cost_estimate=flops and pl.CostEstimate(flops=flops, bytes_accessed=12000000, transcendentals=0),
        input_output_aliases=aliases or {},
        compiler_params=pltpu.CompilerParams(vmem_limit_bytes=LIMIT),
    )(*scalars, *arrays)


def bf16(*shape):
    return jax.ShapeDtypeStruct(shape, jnp.bfloat16)


def shift(x, axis, size, step):
    return lax.ppermute(x, axis, [(i, (i + step) % size) for i in range(size)])


def mirrored(x, axis, size, step):
    pairs = []
    for i in range(size):
        pairs.append((i * NC, (i + step) % size * NC))
        pairs.append((i * NC + 1, (i - step) % size * NC + 1))
    return lax.ppermute(x, (axis, "core"), pairs)


def swap_cores(x):
    return shift(x, "core", NC, 1)


def pick_kernel(info, *refs):
    gathered, out = refs[:NY], refs[NY]
    counted, y = info[SLOTS], info[SLOTS + 1]
    for s in range(SLOTS):
        column = info[s]
        z_at, y_at = lax.div(column, NY), lax.rem(column, NY)
        from_y = lax.rem(y - y_at + NY, NY)
        rows = gathered[0][z_at]
        for d in range(1, NY):
            rows = jnp.where(from_y == d, gathered[d][z_at], rows)
        out[s] = jnp.where(s < counted, rows, jnp.zeros_like(rows))


def load_kernel(source, out, done):
    copy = pltpu.make_async_copy(source, out, done)
    copy.start()
    copy.wait()


def load(source):
    return pl.pallas_call(
        load_kernel,
        out_shape=jax.ShapeDtypeStruct(source.shape, source.dtype),
        in_specs=[pl.BlockSpec(memory_space=pl.ANY)],
        out_specs=VMEM,
        scratch_shapes=[pltpu.SemaphoreType.DMA],
        compiler_params=pltpu.CompilerParams(vmem_limit_bytes=LIMIT),
    )(source)


def half(core, integrals, mine, other):
    first = core[0] == 0
    left = jnp.concatenate(
        [integrals[s].reshape(ROWS, BLOCK) for s in range(SLOTS)], axis=1
    )
    parts = []
    for m, o in zip(mine, other):
        a, b = m[...], o[...]
        top, low = jnp.where(first, a, b), jnp.where(first, b, a)
        parts.append(jnp.concatenate([top, low], axis=1).reshape(SLOTS * BLOCK, SLICE))
    right = parts[0] if len(parts) == 1 else jnp.concatenate(parts, axis=1)
    return jnp.dot(left, right, preferred_element_type=jnp.float32).astype(jnp.bfloat16)


def half_kernel(core, integrals, *refs):
    (*slices, out), earlier = (refs, None) if len(refs) == 5 else (refs[:4] + refs[5:6], refs[4])
    done = half(core, integrals, slices[:2], slices[2:])
    for p in range(AUX_HERE):
        at = slice(p * 2 * SLICE, (p + 1) * 2 * SLICE)
        out[0, :, at] = done[p * BLOCK:(p + 1) * BLOCK]
        if earlier is not None:
            refs[6][1, :, at] = done[p * BLOCK:(p + 1) * BLOCK]
    if earlier is not None:
        refs[6][0] = earlier[0]


def place_of(place, offset):
    z, core = place[0], place[2]
    at = lax.rem(z + offset + NZ, NZ)
    return lax.div(at, NC), lax.rem(lax.rem(at, NC) + core, NC)


def times(rows, columns):
    return lax.dot_general(
        rows, columns, (((1,), (1,)), ((), ())), preferred_element_type=jnp.float32
    )


def row_places(place):
    y, sign = place[1], 1 - 2 * place[2]
    return [y] + [lax.rem(y + d * sign + NY, NY) for d in (-1, 1, 2)]


def put(place, out, total, offsets):
    row_at = row_places(place)
    for n, offset in enumerate(offsets):
        x_at, side = place_of(place, offset)
        for r in range(NY):
            at = row_at[r] * NX + x_at
            out[side, at] = total[r * BLOCK:(r + 1) * BLOCK, n * BLOCK:(n + 1) * BLOCK]


def product(grows, blocks):
    total = None
    for h in range(2):
        rows = jnp.concatenate([g[h] for g in grows], axis=0)
        columns = [block[h][0] for block in blocks]
        columns = columns[0] if len(columns) == 1 else jnp.concatenate(columns, axis=0)
        term = times(rows, columns)
        total = term if total is None else total + term
    return total


def first_kernel(place, *refs):
    grows, out = refs[:4], refs[4]
    own = grows[0]
    put(place, out, product(grows, [(own.at[pl.ds(0, 1)], own.at[pl.ds(1, 1)])]), (0,))


def early_kernel(place, *refs):
    grows, columns, out = refs[:4], refs[4:12], refs[13]
    blocks = [columns[2 * n:2 * n + 2] for n in range(4)]
    put(place, out, product(grows, blocks), (-1, 1, -2, 2))


def late_kernel(place, *refs):
    grows, columns, out = refs[:4], refs[4:12], refs[13]
    put(place, out, product(grows, [columns[0:2], columns[2:4]]), (-3, 3))
    total = None
    for h in range(2):
        rows = jnp.concatenate([g[h] for g in grows], axis=0)
        block = jnp.concatenate([columns[4 + 2 * h][0], columns[5 + 2 * h][0]], axis=0)
        term = times(rows, block)
        total = term if total is None else total + term
    put(place, out, total, (4,))


def encode_kernel(kept, got, out):
    for n in range(NY * NX):
        total = kept[0, n] + got[n]
        top = jnp.maximum(jnp.max(jnp.abs(total), axis=0, keepdims=True), 2.0 ** -120)
        power = jnp.ceil(jnp.log2(top))
        scaled = jnp.floor(total * jnp.exp2(-power) * STEPS + 0.5)
        out[n, :BLOCK] = scaled.astype(jnp.int32).astype(jnp.int16)
        power = jnp.broadcast_to(power, (PAD, BLOCK))
        out[n, BLOCK:] = power.astype(jnp.int32).astype(jnp.int16)


def finish_kernel(parts, out):
    scale = 1.0 / math.sqrt(AUX_HERE * NX * NC * NOCC) / STEPS
    for yy in range(NY):
        total = None
        for xx in range(NX):
            part = parts.at[yy * NX + xx]
            power = part[BLOCK:].astype(jnp.int32).astype(jnp.float32)[:1]
            term = part[:BLOCK].astype(jnp.int32).astype(jnp.float32) * (jnp.exp2(power) * scale)
            total = term if total is None else total + term
        out[:, yy * BLOCK:(yy + 1) * BLOCK] = total


def shards(pair_cols, pair_count, integrals, coeffs):
    z, y = lax.axis_index("z"), lax.axis_index("y")
    x, core = lax.axis_index("x"), lax.axis_index("core")
    core_at = core[None].astype(jnp.int32)
    place = jnp.stack([z, y, core]).astype(jnp.int32)

    info = jnp.concatenate([pair_cols[0], pair_count, y[None].astype(jnp.int32)])
    loaded = load(integrals)

    piece = lax.dynamic_slice(coeffs, (core * HALF_L, x * SLICE), (HALF_L, SLICE))
    along_z = lax.all_to_all(
        jnp.broadcast_to(piece[None], (NZ, HALF_L, SLICE)), "z", 0, 0, tiled=True
    )
    along_z, loaded, info = lax.optimization_barrier((along_z, loaded, info))
    gathered = [along_z] + [shift(along_z, "y", NY, d) for d in (1, 2, 3)]
    picked = call(
        pick_kernel, bf16(SLOTS, HALF_L, SLICE),
        [info], gathered,
    )
    slices = [picked] + [shift(picked, "x", NX, d) for d in (1, 3, 2)]
    others = [swap_cores(m) for m in slices]
    chunk = bf16(1, BLOCK, 2 * CHUNK)
    near = call(half_kernel, chunk, [core_at], [loaded] + slices[:2] + others[:2], flops=530000000)
    far, halfway = call(
        half_kernel, (chunk, bf16(2, BLOCK, 2 * CHUNK)), [core_at],
        [loaded] + slices[2:] + others[2:] + [near],
    )
    halves = [near, far]
    ups, downs = list(halves), list(halves)
    y_a, y_b = mirrored(halfway, "y", NY, 1), mirrored(halfway, "y", NY, -1)
    y_far = mirrored(y_a, "y", NY, 1)
    columns = []
    for step in range(3):
        for h in range(2):
            up, down = shift(ups[h], "z", NZ, 1), shift(downs[h], "z", NZ, -1)
            if h == 1 and step == 1:
                up, down, y_a, y_b = lax.optimization_barrier((up, down, y_a, y_b))
            ups[h], downs[h] = up, down
        columns.append([(ups[0], ups[1]), (downs[0], downs[1])])
    last = []
    for h in range(2):
        low = shift(ups[h][:, :BLOCK // 2], "z", NZ, 1)
        high = shift(downs[h][:, BLOCK // 2:], "z", NZ, -1)
        last.append((low, high))
    rows = [halfway, y_a, y_b, y_far]

    tiles = jax.ShapeDtypeStruct((NC, NY * NX, BLOCK, BLOCK), jnp.float32)
    def blocks(pairs):
        return [half for pair in pairs for half in pair]

    tile = call(first_kernel, tiles, [place], rows, flops=270000000)
    tile = call(
        early_kernel, tiles, [place], rows + blocks(columns[0] + columns[1]) + [tile],
        flops=1080000000, aliases={13: 0},
    )
    tile = call(late_kernel, tiles, [place], rows + blocks(columns[2] + last) + [tile], aliases={13: 0})

    coded = call(
        encode_kernel, jax.ShapeDtypeStruct((NY * NX, BLOCK + PAD, BLOCK), jnp.int16), [],
        [tile, swap_cores(tile[1])],
    )
    parts = lax.all_to_all(coded, ("y", "x"), 0, 0, tiled=True)
    return call(
        finish_kernel, jax.ShapeDtypeStruct((BLOCK, NY * BLOCK), jnp.float32), [], [parts]
    )


def solution(mesh):
    grid = Mesh(mesh.devices.reshape(NZ, NY, NX, NC), ("z", "y", "x", "core"))
    blk, aux = ("z", "y"), ("x", "core")
    placed = (P(blk, None), P(blk), P(blk, aux, None, None), P(blk, None))
    return jax.shard_map(
        shards, mesh=grid, in_specs=placed, out_specs=P(blk, aux), check_vma=False
    )
```

```python
import functools
import math

import jax
import jax.numpy as jnp
from jax import lax
from jax.experimental import pallas as pl
from jax.experimental.pallas import tpu as pltpu
from jax.sharding import Mesh, PartitionSpec as P

NZ, NY, NX, NC = 8, 4, 4, 2
SLOTS, BLOCK, NOCC, AUX_HERE = 16, 128, 512, 4
HALF_L = BLOCK // NC
SLICE = NOCC // NX
CHUNK = AUX_HERE * SLICE
ROWS = AUX_HERE * BLOCK
STEPS, PAD = 32000.0, 16
LIMIT = 24 * 1024 * 1024
VMEM = pl.BlockSpec(memory_space=pltpu.VMEM)
SMEM = pl.BlockSpec(memory_space=pltpu.SMEM)


def call(body, out_shape, scalars, arrays, flops=None, aliases=None):
    return pl.pallas_call(
        body,
        out_shape=out_shape,
        in_specs=[SMEM] * len(scalars) + [VMEM] * len(arrays),
        out_specs=jax.tree.map(lambda _: VMEM, out_shape),
        cost_estimate=flops and pl.CostEstimate(flops=flops, bytes_accessed=12000000, transcendentals=0),
        input_output_aliases=aliases or {},
        compiler_params=pltpu.CompilerParams(vmem_limit_bytes=LIMIT),
    )(*scalars, *arrays)


def bf16(*shape):
    return jax.ShapeDtypeStruct(shape, jnp.bfloat16)


def shift(x, axis, size, step):
    return lax.ppermute(x, axis, [(i, (i + step) % size) for i in range(size)])


def mirrored(x, axis, size, step):
    pairs = []
    for i in range(size):
        pairs.append((i * NC, (i + step) % size * NC))
        pairs.append((i * NC + 1, (i - step) % size * NC + 1))
    return lax.ppermute(x, (axis, "core"), pairs)


def swap_cores(x):
    return shift(x, "core", NC, 1)


def pick_kernel(info, *refs):
    gathered, out = refs[:NY], refs[NY]
    counted, y = info[SLOTS], info[SLOTS + 1]
    for s in range(SLOTS):
        column = info[s]
        z_at, y_at = lax.div(column, NY), lax.rem(column, NY)
        from_y = lax.rem(y - y_at + NY, NY)
        rows = gathered[0][z_at]
        for d in range(1, NY):
            rows = jnp.where(from_y == d, gathered[d][z_at], rows)
        out[s] = jnp.where(s < counted, rows, jnp.zeros_like(rows))


def load_kernel(source, out, done):
    copy = pltpu.make_async_copy(source, out, done)
    copy.start()
    copy.wait()


def load(source):
    return pl.pallas_call(
        load_kernel,
        out_shape=jax.ShapeDtypeStruct(source.shape, source.dtype),
        in_specs=[pl.BlockSpec(memory_space=pl.ANY)],
        out_specs=VMEM,
        scratch_shapes=[pltpu.SemaphoreType.DMA],
        compiler_params=pltpu.CompilerParams(vmem_limit_bytes=LIMIT),
    )(source)


def half(core, integrals, mine, other):
    first = core[0] == 0
    left = jnp.concatenate(
        [integrals[s].reshape(ROWS, BLOCK) for s in range(SLOTS)], axis=1
    )
    parts = []
    for m, o in zip(mine, other):
        a, b = m[...], o[...]
        top, low = jnp.where(first, a, b), jnp.where(first, b, a)
        parts.append(jnp.concatenate([top, low], axis=1).reshape(SLOTS * BLOCK, SLICE))
    right = parts[0] if len(parts) == 1 else jnp.concatenate(parts, axis=1)
    return jnp.dot(left, right, preferred_element_type=jnp.float32).astype(jnp.bfloat16)


def half_kernel(core, integrals, *refs):
    (*slices, out), earlier = (refs, None) if len(refs) == 5 else (refs[:4] + refs[5:6], refs[4])
    done = half(core, integrals, slices[:2], slices[2:])
    for p in range(AUX_HERE):
        at = slice(p * 2 * SLICE, (p + 1) * 2 * SLICE)
        out[0, :, at] = done[p * BLOCK:(p + 1) * BLOCK]
        if earlier is not None:
            refs[6][0, :, at] = done[p * BLOCK:(p + 1) * BLOCK]
    if earlier is not None:
        refs[6][1] = earlier[0]


def place_of(place, offset):
    z, core = place[0], place[2]
    at = lax.rem(z + offset + NZ, NZ)
    return lax.div(at, NC), lax.rem(lax.rem(at, NC) + core, NC)


def times(rows, columns):
    return lax.dot_general(
        rows, columns, (((1,), (1,)), ((), ())), preferred_element_type=jnp.float32
    )


def row_places(place):
    y, sign = place[1], 1 - 2 * place[2]
    return [y] + [lax.rem(y + d * sign + NY, NY) for d in (-1, 1, 2)]


def put(place, out, total, offsets):
    row_at = row_places(place)
    for n, offset in enumerate(offsets):
        x_at, side = place_of(place, offset)
        for r in range(NY):
            at = row_at[r] * NX + x_at
            out[side, at] = total[r * BLOCK:(r + 1) * BLOCK, n * BLOCK:(n + 1) * BLOCK]


def product(grows, blocks):
    total = None
    for h in range(2):
        rows = jnp.concatenate([g[h] for g in grows], axis=0)
        columns = [block[h][0] for block in blocks]
        columns = columns[0] if len(columns) == 1 else jnp.concatenate(columns, axis=0)
        term = times(rows, columns)
        total = term if total is None else total + term
    return total


def first_kernel(place, *refs):
    grows, out = refs[:4], refs[4]
    own = grows[0]
    put(place, out, product(grows, [(own.at[pl.ds(0, 1)], own.at[pl.ds(1, 1)])]), (0,))


def early_kernel(place, *refs):
    grows, columns, out = refs[:4], refs[4:12], refs[13]
    blocks = [columns[2 * n:2 * n + 2] for n in range(4)]
    put(place, out, product(grows, blocks), (-1, 1, -2, 2))


def late_kernel(place, *refs):
    grows, columns, out = refs[:4], refs[4:12], refs[13]
    put(place, out, product(grows, [columns[0:2], columns[2:4]]), (-3, 3))
    total = None
    for h in range(2):
        rows = jnp.concatenate([g[h] for g in grows], axis=0)
        block = jnp.concatenate([columns[4 + 2 * h][0], columns[5 + 2 * h][0]], axis=0)
        term = times(rows, block)
        total = term if total is None else total + term
    put(place, out, total, (4,))


def encode_kernel(kept, got, out):
    for n in range(NY * NX):
        total = kept[0, n] + got[n]
        top = jnp.maximum(jnp.max(jnp.abs(total), axis=0, keepdims=True), 2.0 ** -120)
        power = jnp.ceil(jnp.log2(top))
        scaled = jnp.floor(total * jnp.exp2(-power) * STEPS + 0.5)
        out[n, :BLOCK] = scaled.astype(jnp.int32).astype(jnp.int16)
        power = jnp.broadcast_to(power, (PAD, BLOCK))
        out[n, BLOCK:] = power.astype(jnp.int32).astype(jnp.int16)


def finish_kernel(parts, out):
    scale = 1.0 / math.sqrt(AUX_HERE * NX * NC * NOCC) / STEPS
    for yy in range(NY):
        total = None
        for xx in range(NX):
            part = parts.at[yy * NX + xx]
            power = part[BLOCK:].astype(jnp.int32).astype(jnp.float32)[:1]
            term = part[:BLOCK].astype(jnp.int32).astype(jnp.float32) * (jnp.exp2(power) * scale)
            total = term if total is None else total + term
        out[:, yy * BLOCK:(yy + 1) * BLOCK] = total


def shards(pair_cols, pair_count, integrals, coeffs):
    z, y = lax.axis_index("z"), lax.axis_index("y")
    x, core = lax.axis_index("x"), lax.axis_index("core")
    core_at = core[None].astype(jnp.int32)
    place = jnp.stack([z, y, core]).astype(jnp.int32)

    info = jnp.concatenate([pair_cols[0], pair_count, y[None].astype(jnp.int32)])
    loaded = load(integrals)

    piece = lax.dynamic_slice(coeffs, (core * HALF_L, x * SLICE), (HALF_L, SLICE))
    along_z = lax.all_to_all(
        jnp.broadcast_to(piece[None], (NZ, HALF_L, SLICE)), "z", 0, 0, tiled=True
    )
    along_z, loaded, info = lax.optimization_barrier((along_z, loaded, info))
    gathered = [along_z] + [shift(along_z, "y", NY, d) for d in (1, 2, 3)]
    picked = call(
        pick_kernel, bf16(SLOTS, HALF_L, SLICE),
        [info], gathered,
    )
    slices = [picked] + [shift(picked, "x", NX, d) for d in (1, 3, 2)]
    others = [swap_cores(m) for m in slices]
    chunk = bf16(1, BLOCK, 2 * CHUNK)
    near = call(half_kernel, chunk, [core_at], [loaded] + slices[:2] + others[:2], flops=530000000)
    far, halfway = call(
        half_kernel, (chunk, bf16(2, BLOCK, 2 * CHUNK)), [core_at],
        [loaded] + slices[2:] + others[2:] + [near],
    )
    halves = [far, near]
    ups, downs = list(halves), list(halves)
    y_a, y_b = mirrored(halfway, "y", NY, 1), mirrored(halfway, "y", NY, -1)
    y_far = mirrored(y_a, "y", NY, 1)
    columns = []
    for step in range(3):
        for h in range(2):
            up, down = shift(ups[h], "z", NZ, 1), shift(downs[h], "z", NZ, -1)
            if h == 1 and step == 1:
                up, down, y_b = lax.optimization_barrier((up, down, y_b))
            ups[h], downs[h] = up, down
        columns.append([(ups[0], ups[1]), (downs[0], downs[1])])
    last = []
    for h in range(2):
        low = shift(ups[h][:, :BLOCK // 2], "z", NZ, 1)
        high = shift(downs[h][:, BLOCK // 2:], "z", NZ, -1)
        last.append((low, high))
    rows = [halfway, y_a, y_b, y_far]

    tiles = jax.ShapeDtypeStruct((NC, NY * NX, BLOCK, BLOCK), jnp.float32)
    def blocks(pairs):
        return [half for pair in pairs for half in pair]

    tile = call(first_kernel, tiles, [place], rows, flops=270000000)
    tile = call(
        early_kernel, tiles, [place], rows + blocks(columns[0] + columns[1]) + [tile],
        flops=1080000000, aliases={13: 0},
    )
    tile = call(late_kernel, tiles, [place], rows + blocks(columns[2] + last) + [tile], aliases={13: 0})

    coded = call(
        encode_kernel, jax.ShapeDtypeStruct((NY * NX, BLOCK + PAD, BLOCK), jnp.int16), [],
        [tile, swap_cores(tile[1])],
    )
    parts = lax.all_to_all(coded, ("y", "x"), 0, 0, tiled=True)
    return call(
        finish_kernel, jax.ShapeDtypeStruct((BLOCK, NY * BLOCK), jnp.float32), [], [parts]
    )


def solution(mesh):
    grid = Mesh(mesh.devices.reshape(NZ, NY, NX, NC), ("z", "y", "x", "core"))
    blk, aux = ("z", "y"), ("x", "core")
    placed = (P(blk, None), P(blk), P(blk, aux, None, None), P(blk, None))
    return jax.shard_map(
        shards, mesh=grid, in_specs=placed, out_specs=P(blk, aux), check_vma=False
    )
```
